512 devices in a mesh: ep: 64 (over x_hi, z, core), edp: 8 (over x_lo, y).
Axes of the slice: x: 4 (x_hi: 2, x_lo: 2; x = x_hi * 2 + x_lo), y: 4, z: 16, core: 2. Of those that a mesh axis runs over, the one named last changes fastest.
Arguments:
- dense_acts: bfloat16 [327680, 512], P(('ep', 'edp')), may hold values from -6 to 6
- dense_cot: bfloat16 [327680, 1536], P(('ep', 'edp')), may hold values from -6 to 6
- advantage: float32 [327680], P(('ep', 'edp')), may hold values from -5 to 5
- dense_master: float32 [512, 1536], P(('ep', 'edp')), may hold values from -0.6 to 0.6
- dense_first: float32 [512, 1536], P(('ep', 'edp')), may hold values from -0.1 to 0.1
- dense_second: float32 [512, 1536], P(('ep', 'edp')), may hold values from 0.002 to 0.1
- routed_grads: bfloat16 [8, 256, 8, 2048], P('edp', 'ep'), may hold values from -6 to 6
- routed_master: float32 [256, 8, 2048], P('ep', 'edp'), may hold values from -0.6 to 0.6
- routed_first: float32 [256, 8, 2048], P('ep', 'edp'), may hold values from -0.1 to 0.1
- routed_second: float32 [256, 8, 2048], P('ep', 'edp'), may hold values from 0.002 to 0.1
Outputs:
- dense_master_new: float32 [512, 1536], P(('ep', 'edp'))
- dense_first_new: float32 [512, 1536], P(('ep', 'edp'))
- dense_second_new: float32 [512, 1536], P(('ep', 'edp'))
- dense_weights: bfloat16 [512, 1536], replicated
- routed_master_new: float32 [256, 8, 2048], P('ep', 'edp')
- routed_first_new: float32 [256, 8, 2048], P('ep', 'edp')
- routed_second_new: float32 [256, 8, 2048], P('ep', 'edp')
- routed_weights: bfloat16 [256, 8, 2048], P('ep')
The draws below stay inside these ranges and needn't reach their ends.
All inputs are finite; a program needn't handle non-finite values.
Results may differ from the reference program's by a relative error of at most 0.0034.
Values may be sent and summed in bfloat16 or wider, within the bound.
No kernel may reach another device: no remote copies, remote signals or barrier semaphores. Data moves between devices by JAX's collectives and lax.ppermute only.
A program may use at most 64 MiB of HBM per device.

```python
import math
import jax
import jax.numpy as jnp
from jax import lax

FF = 2048
QR = 1536
ER = 8
DR = 512
EXPERTS = 256
TOKENS = 327680
N_EP = 64
N_EDP = 8


def strengthened(array, key, source, target, shards_of, factor):
    owner, partner = [(jnp.arange(array.shape[dim]) // (array.shape[dim] // shards_of)).reshape([-1 if axis == dim else 1 for axis in range(array.ndim)]) for dim in (source, target)]
    chosen = jax.random.permutation(key, shards_of)[partner]
    strong = (owner == chosen) | (owner == (partner + shards_of // 2) % shards_of)
    return jnp.where(strong, factor * array, array)


def level_of(own_key, extent, shards, least, top_value):
    level, own = 1.0, jax.random.fold_in(own_key, 6)
    for axis_at, shards_of in shards:
        heights = jnp.exp(jax.random.uniform(jax.random.fold_in(own, axis_at), (shards_of,), jnp.float32, least / len(shards), top_value / len(shards)))
        level = level * jnp.repeat(heights, extent[axis_at] // shards_of).reshape([-1 if axis == axis_at else 1 for axis in range(len(extent))])
    return level


def bell_draw(own_key, dims, deviation, bound, pieces=(), kind=jnp.bfloat16):
    gain = level_of(own_key, dims, pieces, -0.22, 0.18) if pieces else 1.0
    result = jax.random.normal(own_key, dims, jnp.float32) * deviation * gain
    return jnp.minimum(jnp.maximum(result, -bound), bound).astype(kind)


def bell_draw_with(stream_key, extent, deviation, reach, shards, heavy, kind=jnp.bfloat16):
    array = deviation * jax.random.normal(stream_key, extent, jnp.float32)
    if shards:
        array = array * level_of(stream_key, extent, shards, -0.22, 0.18)
    return jnp.clip(strengthened(array, jax.random.fold_in(stream_key, 3), *heavy), -reach, reach).astype(kind)


def setup_inputs(seed: int = 0) -> dict:
    splits = jax.random.split(jax.random.key(seed), 11)
    return {
        "dense_acts": bell_draw(splits[0], (TOKENS, DR), 1.0, 6.0, ((0, 512),)),
        "dense_cot": bell_draw(splits[1], (TOKENS, QR), 1.0, 6.0, ((0, 512),)),
        "advantage": bell_draw(splits[2], (TOKENS,), 1.0, 5.0, ((0, 512),), jnp.float32),
        "dense_master": bell_draw(splits[3], (DR, QR), 0.1, 0.6, ((0, 512),), jnp.float32),
        "dense_first": bell_draw(splits[4], (DR, QR), 0.02, 0.1, ((0, 512),), jnp.float32),
        "dense_second": jnp.clip(jnp.exp(math.log(0.1) - 3.912023 * jax.random.uniform(splits[5], (DR, QR), jnp.float32) ** level_of(splits[5], (DR, QR), ((0, 512),), -0.2, 0.2)), 0.002, 0.1),
        "routed_grads": bell_draw_with(splits[6], (N_EDP, EXPERTS, ER, FF), 0.5, 6.0, ((0, 8), (1, 64)), (0, 2, 8, 2.0)),
        "routed_master": bell_draw(splits[7], (EXPERTS, ER, FF), 0.1, 0.6, ((0, 64), (1, 8)), jnp.float32),
        "routed_first": bell_draw(splits[8], (EXPERTS, ER, FF), 0.02, 0.1, ((0, 64), (1, 8)), jnp.float32),
        "routed_second": jnp.clip(jnp.exp(math.log(0.1) - 3.912023 * jax.random.uniform(splits[9], (EXPERTS, ER, FF), jnp.float32) ** level_of(splits[9], (EXPERTS, ER, FF), ((0, 64), (1, 8)), -0.2, 0.2)), 0.002, 0.1),
    }


beta_one = 0.9
beta_two = 0.95
learn_rate = 0.001
decay_rate = 0.1
epsilon = 1e-08

def adamw_update(gradient, master, first_moment, second_moment):
    first_new = beta_one * first_moment + (1.0 - beta_one) * gradient
    second_new = beta_two * second_moment + (1.0 - beta_two) * gradient * gradient
    master_new = master - learn_rate * (first_new / (jnp.sqrt(second_new) + epsilon) + decay_rate * master)
    return (master_new, first_new, second_new)

def reference(dense_acts, dense_cot, advantage, dense_master, dense_first, dense_second, routed_grads, routed_master, routed_first, routed_second):
    acts_blocks = dense_acts.reshape(N_EP, TOKENS // N_EP, DR)
    cot_blocks = dense_cot.reshape(N_EP, TOKENS // N_EP, QR)
    weight_blocks = advantage.reshape(N_EP, TOKENS // N_EP)

    def accumulate(running, block):
        acts_here, cot_here, weight_here = block
        scaled = (weight_here[:, None] * cot_here.astype(jnp.float32)).astype(jnp.bfloat16)
        return (running + jnp.dot(acts_here.T, scaled, preferred_element_type=jnp.float32), None)
    summed, unused = lax.scan(accumulate, jnp.zeros((DR, QR), jnp.float32), (acts_blocks, cot_blocks, weight_blocks))
    dense_grad = summed * (1.0 / math.sqrt(TOKENS))
    routed_grad = lax.optimization_barrier(jnp.sum(routed_grads.astype(jnp.float32), axis=0))
    dense_master_new, dense_first_new, dense_second_new = adamw_update(dense_grad, dense_master, dense_first, dense_second)
    routed_master_new, routed_first_new, routed_second_new = adamw_update(routed_grad, routed_master, routed_first, routed_second)
    return (dense_master_new, dense_first_new, dense_second_new, dense_master_new.astype(jnp.bfloat16), routed_master_new, routed_first_new, routed_second_new, routed_master_new.astype(jnp.bfloat16))
```

```python
import math

import jax
import jax.numpy as jnp
from jax import lax
from jax.sharding import Mesh, PartitionSpec as P

beta_one = 0.9
beta_two = 0.95
learn_rate = 0.001
decay_rate = 0.1
epsilon = 1e-08

AXES = ("xh", "z", "core", "xl", "y")
SIZES = (2, 16, 2, 2, 4)
EP = ("xh", "z", "core")
EDP = ("xl", "y")
FAR = ("xh", "z")


def adamw_update(gradient, master, first_moment, second_moment):
    first_new = beta_one * first_moment + (1.0 - beta_one) * gradient
    second_new = beta_two * second_moment + (1.0 - beta_two) * gradient * gradient
    master_new = master - learn_rate * (
        first_new / (jnp.sqrt(second_new) + epsilon) + decay_rate * master
    )
    return (master_new, first_new, second_new)


def exchange(x, axes):
    return lax.all_to_all(x, axes, 0, 0, tiled=False)


def per_device(
    dense_acts,
    dense_cot,
    advantage,
    dense_master,
    dense_first,
    dense_second,
    routed_grads,
    routed_master,
    routed_first,
    routed_second,
):
    f32, bf16 = jnp.float32, jnp.bfloat16
    rows, columns = dense_acts.shape[1], dense_cot.shape[1]
    n_far, n_edp, n_core = 32, 8, 2
    half = rows // 2
    factor = 1.0 / math.sqrt(dense_acts.shape[0] * 512)
    core = lax.axis_index("core")

    packed = jnp.arange(rows)[None, :]
    which, e, far = packed // half, packed // n_far % n_edp, packed % n_far
    row = (far * n_core + jnp.where(which == 1, core, 1 - core)) * n_edp + e
    place = (jnp.arange(rows)[:, None] == row).astype(bf16)

    acts = lax.dot_general(
        dense_acts, place, (((1,), (0,)), ((), ())), preferred_element_type=bf16
    )
    scaled = (advantage[:, None] * dense_cot.astype(f32)).astype(bf16)

    def product(a):
        return lax.dot_general(a, scaled, (((0,), (0,)), ((), ())), preferred_element_type=f32)

    other = product(acts[:, :half]).astype(bf16)
    received = lax.ppermute(other, "core", [(0, 1), (1, 0)])
    own = product(acts[:, half:])
    summed = (own + received.astype(f32)).astype(bf16).reshape(n_edp, n_far, columns)

    w = 512
    routed = routed_grads[0].transpose(1, 0, 2)
    packs = [summed[:, :, i * w : (i + 1) * w] for i in range(columns // w)]
    packs += [routed[:, :, i * w : (i + 1) * w] for i in range(routed.shape[2] // w)]
    got = exchange(jnp.concatenate(packs, axis=1), EDP)
    total = jnp.sum(got, axis=0, dtype=f32)
    nd = columns // w
    dense_part = jnp.concatenate([total[i * n_far : (i + 1) * n_far] for i in range(nd)], axis=1)
    base = nd * n_far
    routed_grad = jnp.concatenate(
        [total[base + i * 4 : base + (i + 1) * 4] for i in range(routed.shape[2] // w)], axis=1
    )[:, None, :]

    got = exchange(dense_part, FAR)
    dense_grad = jnp.sum(got, axis=0, keepdims=True) * factor
    dense_master_new, dense_first_new, dense_second_new = adamw_update(
        dense_grad, dense_master, dense_first, dense_second
    )
    shard = dense_master_new.astype(bf16)
    routed_master_new, routed_first_new, routed_second_new = adamw_update(
        routed_grad, routed_master, routed_first, routed_second
    )
    shards = exchange(jnp.broadcast_to(shard, (n_far, columns)), FAR)
    rw = routed_master_new.astype(bf16)[:, 0, :]
    mine = jnp.concatenate(
        [shards[:, i * w : (i + 1) * w] for i in range(nd)]
        + [rw[:, i * w : (i + 1) * w] for i in range(routed.shape[2] // w)],
        axis=0,
    )
    got = exchange(jnp.broadcast_to(mine[None], (n_edp,) + mine.shape), EDP)
    own_w = jnp.concatenate([got[:, i * n_far : (i + 1) * n_far] for i in range(nd)], axis=2)
    own_w = own_w.reshape(half, columns)
    other_w = lax.ppermute(own_w, "core", [(0, 1), (1, 0)])
    routed_weights = jnp.concatenate(
        [got[:, base + i * 4 : base + (i + 1) * 4] for i in range(routed.shape[2] // w)], axis=2
    ).transpose(1, 0, 2)
    dense_weights = lax.dot_general(
        place[:, half:], own_w, (((1,), (0,)), ((), ())), preferred_element_type=f32
    ) + lax.dot_general(
        place[:, :half], other_w, (((1,), (0,)), ((), ())), preferred_element_type=f32
    )
    return (
        dense_master_new,
        dense_first_new,
        dense_second_new,
        dense_weights.astype(bf16),
        routed_master_new,
        routed_first_new,
        routed_second_new,
        routed_weights,
    )


def solution(mesh):
    inner = Mesh(mesh.devices.reshape(SIZES), AXES)
    in_specs = (
        P(AXES, None),
        P(AXES, None),
        P(AXES),
        P(AXES, None),
        P(AXES, None),
        P(AXES, None),
        P(EDP, EP, None, None),
        P(EP, EDP, None),
        P(EP, EDP, None),
        P(EP, EDP, None),
    )
    out_specs = (
        P(AXES, None),
        P(AXES, None),
        P(AXES, None),
        P(),
        P(EP, EDP, None),
        P(EP, EDP, None),
        P(EP, EDP, None),
        P(EP, None, None),
    )
    return jax.shard_map(
        per_device, mesh=inner, in_specs=in_specs, out_specs=out_specs, check_vma=False
    )
```

```python
import math

import jax
import jax.numpy as jnp
from jax import lax
from jax.experimental import pallas as pl
from jax.experimental.pallas import tpu as pltpu
from jax.sharding import Mesh, PartitionSpec as P

beta_one = 0.9
beta_two = 0.95
learn_rate = 0.001
decay_rate = 0.1
epsilon = 1e-08

AXES = ("xh", "z", "core", "xl", "y")
SIZES = (2, 16, 2, 2, 4)
EP = ("xh", "z", "core")
EDP = ("xl", "y")
NEAR = ("xh", "xl", "y")
FAR = ("z",)
N_NEAR, N_FAR, N_EDP, N_CORE, N_XH, N_DEV = 16, 16, 8, 2, 2, 512
ROWS, COLUMNS, EXPERTS, FF = 512, 1536, 4, 2048
HALF = ROWS // 2
W = 512
N_DENSE, N_ROUTED = COLUMNS // W, FF // W
DENSE_ROWS = N_DENSE * N_FAR
PACKED_ROWS = DENSE_ROWS + N_ROUTED * EXPERTS
LANES = 128
PIECES = COLUMNS // LANES
PIECE_ROWS = 16
f32, bf16 = jnp.float32, jnp.bfloat16


def adamw_update(gradient, master, first_moment, second_moment):
    first_new = beta_one * first_moment + (1.0 - beta_one) * gradient
    second_new = beta_two * second_moment + (1.0 - beta_two) * gradient * gradient
    master_new = master - learn_rate * (
        first_new / (jnp.sqrt(second_new) + epsilon) + decay_rate * master
    )
    return (master_new, first_new, second_new)


def exchange(x, axes):
    return lax.all_to_all(x, axes, 0, 0, tiled=False)


def iota(shape, dim):
    return lax.broadcasted_iota(jnp.int32, shape, dim)


def call(kernel, out_shape, flops=0, nbytes=1 << 20, scratch=()):
    return pl.pallas_call(
        kernel,
        out_shape=out_shape,
        scratch_shapes=scratch,
        compiler_params=pltpu.CompilerParams(vmem_limit_bytes=24 << 20),
        cost_estimate=pl.CostEstimate(flops=flops, bytes_accessed=nbytes, transcendentals=0),
    )


def pack_kernel(own, received, routed, out):
    for i in range(N_DENSE):
        cols = slice(i * W, (i + 1) * W)
        s = own[:, cols] + received[:, cols].astype(f32)
        out[:, i * N_FAR : (i + 1) * N_FAR, :] = s.astype(bf16).reshape(N_NEAR, N_FAR, W)
    xh = lax.axis_index("xh")
    shape = (N_NEAR * 16, EXPERTS * N_EDP)
    q, c = iota(shape, 0), iota(shape, 1)
    same = (q // 128 == xh) & (q // 16 % N_EDP == c % N_EDP) & (q % EXPERTS == c // N_EDP)
    total = jnp.zeros((N_NEAR * 16, W), f32)
    for b in range(N_ROUTED):
        pick = jnp.where(same & (q // EXPERTS % N_ROUTED == b), 1.0, 0.0).astype(bf16)
        total += jnp.dot(pick, routed[:, b * W : (b + 1) * W], preferred_element_type=f32)
    out[:, DENSE_ROWS:, :] = total.astype(bf16).reshape(N_NEAR, 16, W)


def middle_kernel(got, master, first, second, far_out, master_out, first_out, second_out, weights_out):
    total = jnp.sum(got[...].astype(f32), axis=0)
    pieces = [
        total[i * N_FAR : (i + 1) * N_FAR, j * LANES : (j + 1) * LANES]
        for i in range(N_DENSE)
        for j in range(W // LANES)
    ]
    pieces += [jnp.zeros((N_FAR, LANES), f32)] * (PIECE_ROWS - PIECES)
    far_out[...] = jnp.swapaxes(jnp.stack(pieces, axis=0), 0, 1).astype(bf16)
    rows = []
    for x in range(EXPERTS):
        g = jnp.concatenate(
            [total[DENSE_ROWS + b * EXPERTS + x][None] for b in range(N_ROUTED)], axis=1
        )
        p, m, v = adamw_update(g, master[x], first[x], second[x])
        master_out[x], first_out[x], second_out[x] = p, m, v
        rows.append(p)
    packed = [rows[x][:, b * W : (b + 1) * W] for b in range(N_ROUTED) for x in range(EXPERTS)]
    weights_out[...] = jnp.concatenate(packed, axis=0).astype(bf16)


def update_kernel(factor, got, master, first, second, far_out, master_out, first_out, second_out):
    total = jnp.sum(got[...].astype(f32), axis=0)
    g = jnp.concatenate([total[k : k + 1] for k in range(PIECES)], axis=1) * factor
    p, m, v = adamw_update(g, master[...], first[...], second[...])
    master_out[...], first_out[...], second_out[...] = p, m, v
    pieces = [p[:, k * LANES : (k + 1) * LANES] for k in range(PIECES)]
    pieces += [jnp.zeros((PIECE_ROWS - PIECES, LANES), f32)]
    row = jnp.concatenate(pieces, axis=0).astype(bf16)
    far_out[...] = jnp.broadcast_to(row[None], far_out.shape)


def spread_kernel(got, weights, out):
    rows = jnp.swapaxes(got[...].astype(f32), 0, 1)
    per = W // LANES
    blocks = [
        jnp.concatenate([rows[i * per + j] for j in range(per)], axis=1) for i in range(N_DENSE)
    ]
    block = jnp.concatenate(blocks, axis=0).astype(bf16)
    for d in range(N_NEAR):
        out[d, :DENSE_ROWS, :] = block
        out[d, DENSE_ROWS:, :] = weights[...]


def unpack_kernel(own, other, dense_out, routed_out):
    core, xh = lax.axis_index("core"), lax.axis_index("xh")
    n = HALF
    r, p = iota((n, n), 0), iota((n, n), 1)
    here = r // N_EDP % N_CORE == core
    same = (r // 16 == p % N_FAR) & (r % N_EDP == p // N_FAR % N_EDP) & (here == (p < n // 2))
    place = jnp.where(same, 1.0, 0.0).astype(bf16)
    for x in range(N_XH):
        for i in range(N_DENSE):
            parts = [
                ref[x * N_EDP : (x + 1) * N_EDP, i * N_FAR : (i + 1) * N_FAR, :].reshape(n // 2, W)
                for ref in (own, other)
            ]
            block = jnp.concatenate(parts, axis=0)
            dense_out[x * n : (x + 1) * n, i * W : (i + 1) * W] = jnp.dot(
                place, block, preferred_element_type=f32
            ).astype(bf16)
    shape = (EXPERTS * N_EDP, N_NEAR * 16)
    c, q = iota(shape, 0), iota(shape, 1)
    same = (q // 128 == xh) & (q // 16 % N_EDP == c % N_EDP) & (q % EXPERTS == c // N_EDP)
    packed = own[:, DENSE_ROWS:, :].reshape(N_NEAR * 16, W)
    for b in range(N_ROUTED):
        pick = jnp.where(same & (q // EXPERTS % N_ROUTED == b), 1.0, 0.0).astype(bf16)
        routed_out[:, b * W : (b + 1) * W] = jnp.dot(
            pick, packed, preferred_element_type=f32
        ).astype(bf16)


def per_device(
    dense_acts,
    dense_cot,
    advantage,
    dense_master,
    dense_first,
    dense_second,
    routed_grads,
    routed_master,
    routed_first,
    routed_second,
):
    factor = 1.0 / math.sqrt(dense_acts.shape[0] * N_DEV)
    core = lax.axis_index("core")
    sds = jax.ShapeDtypeStruct

    packed = jnp.arange(ROWS)[None, :]
    which, xh, e, z = packed // HALF, packed // 128 % N_XH, packed // N_FAR % N_EDP, packed % N_FAR
    row = ((xh * N_FAR + z) * N_CORE + jnp.where(which == 1, core, 1 - core)) * N_EDP + e
    place = (jnp.arange(ROWS)[:, None] == row).astype(bf16)

    acts = lax.dot_general(
        dense_acts, place, (((1,), (0,)), ((), ())), preferred_element_type=bf16
    )
    scaled = (advantage[:, None] * dense_cot.astype(f32)).astype(bf16)

    def product(a):
        return lax.dot_general(a, scaled, (((0,), (0,)), ((), ())), preferred_element_type=f32)

    swap = [(0, 1), (1, 0)]
    received = lax.ppermute(product(acts[:, :HALF]).astype(bf16), "core", swap)
    own = product(acts[:, HALF:])
    near = sds((N_NEAR, PACKED_ROWS, W), bf16)
    far = sds((N_FAR, PIECE_ROWS, LANES), bf16)
    rows_r = sds((EXPERTS, 1, FF), f32)
    rows_d = sds((1, COLUMNS), f32)
    sent = call(pack_kernel, near)(own, received, routed_grads.reshape(EXPERTS * N_EDP, FF))
    got = exchange(sent, NEAR)
    far_sent, routed_master_new, routed_first_new, routed_second_new, weights = call(
        middle_kernel, (far, rows_r, rows_r, rows_r, sds((16, W), bf16))
    )(got, routed_master, routed_first, routed_second)
    got = exchange(far_sent, FAR)

    def update(*refs):
        update_kernel(factor, *refs)

    far_sent, dense_master_new, dense_first_new, dense_second_new = call(
        update, (far, rows_d, rows_d, rows_d)
    )(got, dense_master, dense_first, dense_second)
    got = exchange(far_sent, FAR)
    own = exchange(call(spread_kernel, near)(got, weights), NEAR)
    other = lax.ppermute(own, "core", swap)
    dense_weights, routed_weights = call(
        unpack_kernel, (sds((ROWS, COLUMNS), bf16), sds((EXPERTS * N_EDP, FF), bf16))
    )(own, other)
    return (
        dense_master_new,
        dense_first_new,
        dense_second_new,
        dense_weights,
        routed_master_new,
        routed_first_new,
        routed_second_new,
        routed_weights.reshape(EXPERTS, N_EDP, FF),
    )


def solution(mesh):
    inner = Mesh(mesh.devices.reshape(SIZES), AXES)
    in_specs = (
        P(AXES, None),
        P(AXES, None),
        P(AXES),
        P(AXES, None),
        P(AXES, None),
        P(AXES, None),
        P(EDP, EP, None, None),
        P(EP, EDP, None),
        P(EP, EDP, None),
        P(EP, EDP, None),
    )
    out_specs = (
        P(AXES, None),
        P(AXES, None),
        P(AXES, None),
        P(),
        P(EP, EDP, None),
        P(EP, EDP, None),
        P(EP, EDP, None),
        P(EP, None, None),
    )
    return jax.shard_map(
        per_device, mesh=inner, in_specs=in_specs, out_specs=out_specs, check_vma=False
    )
```

```python
import math

import jax
import jax.numpy as jnp
from jax import lax
from jax.experimental import pallas as pl
from jax.experimental.pallas import tpu as pltpu
from jax.sharding import Mesh, PartitionSpec as P

beta_one = 0.9
beta_two = 0.95
learn_rate = 0.001
decay_rate = 0.1
epsilon = 1e-08

AXES = ("xh", "z", "core", "xl", "y")
SIZES = (2, 16, 2, 2, 4)
EP = ("xh", "z", "core")
EDP = ("xl", "y")
NEAR = ("xh", "xl", "y")
FAR = ("z",)
N_NEAR, N_FAR, N_EDP, N_CORE, N_XH, N_DEV = 16, 16, 8, 2, 2, 512
ROWS, COLUMNS, EXPERTS, FF = 512, 1536, 4, 2048
HALF = ROWS // 2
W = 512
N_DENSE, N_ROUTED = COLUMNS // W, FF // W
DENSE_ROWS = N_DENSE * N_FAR
PACKED_ROWS = DENSE_ROWS + N_ROUTED * EXPERTS
LANES = 128
PIECES = COLUMNS // LANES
PIECE_ROWS = 16
f32, bf16 = jnp.float32, jnp.bfloat16


def adamw_update(gradient, master, first_moment, second_moment):
    first_new = beta_one * first_moment + (1.0 - beta_one) * gradient
    second_new = beta_two * second_moment + (1.0 - beta_two) * gradient * gradient
    master_new = master - learn_rate * (
        first_new / (jnp.sqrt(second_new) + epsilon) + decay_rate * master
    )
    return (master_new, first_new, second_new)


def exchange(x, axes):
    return lax.all_to_all(x, axes, 0, 0, tiled=False)


def iota(shape, dim):
    return lax.broadcasted_iota(jnp.int32, shape, dim)


def call(kernel, out_shape, flops=0, nbytes=1 << 20, scratch=()):
    return pl.pallas_call(
        kernel,
        out_shape=out_shape,
        scratch_shapes=scratch,
        compiler_params=pltpu.CompilerParams(vmem_limit_bytes=24 << 20),
        cost_estimate=pl.CostEstimate(flops=flops, bytes_accessed=nbytes, transcendentals=0),
    )


def pack_kernel(own, received, routed, out):
    for i in range(N_DENSE):
        cols = slice(i * W, (i + 1) * W)
        s = own[:, cols] + received[:, cols].astype(f32)
        out[:, i * N_FAR : (i + 1) * N_FAR, :] = s.astype(bf16).reshape(N_NEAR, N_FAR, W)
    xh = lax.axis_index("xh")
    shape = (N_NEAR * 16, EXPERTS * N_EDP)
    q, c = iota(shape, 0), iota(shape, 1)
    same = (q // 128 == xh) & (q // 16 % N_EDP == c % N_EDP) & (q % EXPERTS == c // N_EDP)
    total = jnp.zeros((N_NEAR * 16, W), f32)
    for b in range(N_ROUTED):
        pick = jnp.where(same & (q // EXPERTS % N_ROUTED == b), 1.0, 0.0).astype(bf16)
        total += jnp.dot(pick, routed[:, b * W : (b + 1) * W], preferred_element_type=f32)
    out[:, DENSE_ROWS:, :] = total.astype(bf16).reshape(N_NEAR, 16, W)


def middle_kernel(got, master, first, second, far_out, master_out, first_out, second_out, weights_out):
    total = jnp.sum(got[...].astype(f32), axis=0)
    pieces = [
        total[i * N_FAR : (i + 1) * N_FAR, j * LANES : (j + 1) * LANES]
        for i in range(N_DENSE)
        for j in range(W // LANES)
    ]
    pieces += [jnp.zeros((N_FAR, LANES), f32)] * (PIECE_ROWS - PIECES)
    far_out[...] = jnp.swapaxes(jnp.stack(pieces, axis=0), 0, 1).astype(bf16)
    rows = []
    for x in range(EXPERTS):
        g = jnp.concatenate(
            [total[DENSE_ROWS + b * EXPERTS + x][None] for b in range(N_ROUTED)], axis=1
        )
        p, m, v = adamw_update(g, master[x], first[x], second[x])
        master_out[x], first_out[x], second_out[x] = p, m, v
        rows.append(p)
    packed = [rows[x][:, b * W : (b + 1) * W] for b in range(N_ROUTED) for x in range(EXPERTS)]
    weights_out[...] = jnp.concatenate(packed, axis=0).astype(bf16)


def updated(factor, got, master, first, second):
    total = jnp.sum(got[...].astype(f32), axis=0)
    g = jnp.concatenate([total[k : k + 1] for k in range(PIECES)], axis=1) * factor
    return adamw_update(g, master[...], first[...], second[...])


def weights_kernel(factor, got, master, first, second, far_out):
    p = updated(factor, got, master, first, second)[0]
    pieces = [p[:, k * LANES : (k + 1) * LANES] for k in range(PIECES)]
    pieces += [jnp.zeros((PIECE_ROWS - PIECES, LANES), f32)]
    row = jnp.concatenate(pieces, axis=0).astype(bf16)
    far_out[...] = jnp.broadcast_to(row[None], far_out.shape)


def state_kernel(factor, got, master, first, second, master_out, first_out, second_out):
    p, m, v = updated(factor, got, master, first, second)
    master_out[...], first_out[...], second_out[...] = p, m, v


def spread_kernel(got, weights, out):
    rows = jnp.swapaxes(got[...].astype(f32), 0, 1)
    per = W // LANES
    blocks = [
        jnp.concatenate([rows[i * per + j] for j in range(per)], axis=1) for i in range(N_DENSE)
    ]
    block = jnp.concatenate(blocks, axis=0).astype(bf16)
    for d in range(N_NEAR):
        out[d, :DENSE_ROWS, :] = block
        out[d, DENSE_ROWS:, :] = weights[...]


def place_rows(packed, core, out, blocks, sems):
    n = N_EDP * N_FAR
    p, q = iota((n, n), 0), iota((n, n), 1)
    same = (p // N_EDP == q % N_FAR) & (p % N_EDP == q // N_FAR)
    place = jnp.where(same, 1.0, 0.0).astype(bf16)
    copies = []
    for x in range(N_XH):
        for i in range(N_DENSE):
            rows = packed[x * N_EDP : (x + 1) * N_EDP, i * N_FAR : (i + 1) * N_FAR, :]
            block = jnp.dot(place, rows.reshape(n, W), preferred_element_type=f32)
            k = x * N_DENSE + i
            blocks[k] = block.reshape(N_FAR, N_EDP, W).astype(bf16)
            to = out.at[pl.ds(x * N_FAR, N_FAR), core, :, pl.ds(i * W, W)]
            copies.append(pltpu.make_async_copy(blocks.at[k], to, sems.at[k]))
            copies[-1].start()
    return copies


def own_place_kernel(own, dense_out, routed_out, blocks, sems):
    copies = place_rows(own, lax.axis_index("core"), dense_out, blocks, sems)
    xh = lax.axis_index("xh")
    shape = (EXPERTS * N_EDP, N_NEAR * 16)
    c, q = iota(shape, 0), iota(shape, 1)
    same = (q // 128 == xh) & (q // 16 % N_EDP == c % N_EDP) & (q % EXPERTS == c // N_EDP)
    packed = own[:, DENSE_ROWS:, :].reshape(N_NEAR * 16, W)
    for b in range(N_ROUTED):
        pick = jnp.where(same & (q // EXPERTS % N_ROUTED == b), 1.0, 0.0).astype(bf16)
        routed_out[:, b * W : (b + 1) * W] = jnp.dot(
            pick, packed, preferred_element_type=f32
        ).astype(bf16)
    for copy in copies:
        copy.wait()


def other_place_kernel(other, held, dense_out, blocks, sems):
    for copy in place_rows(other, 1 - lax.axis_index("core"), dense_out, blocks, sems):
        copy.wait()


def per_device(
    dense_acts,
    dense_cot,
    advantage,
    dense_master,
    dense_first,
    dense_second,
    routed_grads,
    routed_master,
    routed_first,
    routed_second,
):
    factor = 1.0 / math.sqrt(dense_acts.shape[0] * N_DEV)
    core = lax.axis_index("core")
    sds = jax.ShapeDtypeStruct

    packed = jnp.arange(ROWS)[None, :]
    which, xh, e, z = packed // HALF, packed // 128 % N_XH, packed // N_FAR % N_EDP, packed % N_FAR
    row = ((xh * N_FAR + z) * N_CORE + jnp.where(which == 1, core, 1 - core)) * N_EDP + e
    place = (jnp.arange(ROWS)[:, None] == row).astype(bf16)

    acts = lax.dot_general(
        dense_acts, place, (((1,), (0,)), ((), ())), preferred_element_type=bf16
    )
    scaled = (advantage[:, None] * dense_cot.astype(f32)).astype(bf16)

    def product(a):
        return lax.dot_general(a, scaled, (((0,), (0,)), ((), ())), preferred_element_type=f32)

    swap = [(0, 1), (1, 0)]
    received = lax.ppermute(product(acts[:, :HALF]).astype(bf16), "core", swap)
    own = product(acts[:, HALF:])
    near = sds((N_NEAR, PACKED_ROWS, W), bf16)
    far = sds((N_FAR, PIECE_ROWS, LANES), bf16)
    rows_r = sds((EXPERTS, 1, FF), f32)
    rows_d = sds((1, COLUMNS), f32)
    sent = call(pack_kernel, near)(own, received, routed_grads.reshape(EXPERTS * N_EDP, FF))
    got = exchange(sent, NEAR)
    far_sent, routed_master_new, routed_first_new, routed_second_new, weights = call(
        middle_kernel, (far, rows_r, rows_r, rows_r, sds((16, W), bf16))
    )(got, routed_master, routed_first, routed_second)
    got = exchange(far_sent, FAR)

    def ahead(*refs):
        weights_kernel(factor, *refs)

    def state(*refs):
        state_kernel(factor, *refs)

    dense_args = (got, dense_master, dense_first, dense_second)
    far_sent = call(ahead, far)(*dense_args)
    dense_master_new, dense_first_new, dense_second_new = call(state, (rows_d, rows_d, rows_d))(
        *dense_args
    )
    got = exchange(far_sent, FAR)
    near_sent = call(spread_kernel, near)(got, weights)
    near_sent, dense_master_new, dense_first_new, dense_second_new = lax.optimization_barrier(
        (near_sent, dense_master_new, dense_first_new, dense_second_new)
    )
    own = exchange(near_sent, NEAR)
    other = lax.ppermute(own, "core", swap)
    dense_shape = sds((ROWS // 16, N_CORE, N_EDP, COLUMNS), bf16)
    anywhere = pl.BlockSpec(memory_space=pl.ANY)
    vmem = pl.BlockSpec(memory_space=pltpu.VMEM)
    n_blocks = N_XH * N_DENSE
    place_params = dict(
        scratch_shapes=[
            pltpu.VMEM((n_blocks, N_FAR, N_EDP, W), bf16),
            pltpu.SemaphoreType.DMA((n_blocks,)),
        ],
        compiler_params=pltpu.CompilerParams(vmem_limit_bytes=24 << 20),
        cost_estimate=pl.CostEstimate(flops=200 << 20, bytes_accessed=2 << 20, transcendentals=0),
    )
    held, routed_weights = pl.pallas_call(
        own_place_kernel,
        in_specs=[vmem],
        out_specs=[anywhere, vmem],
        out_shape=(dense_shape, sds((EXPERTS * N_EDP, FF), bf16)),
        **place_params,
    )(own)
    dense_weights = pl.pallas_call(
        other_place_kernel,
        in_specs=[vmem, anywhere],
        out_specs=anywhere,
        out_shape=dense_shape,
        input_output_aliases={1: 0},
        **place_params,
    )(other, held).reshape(ROWS, COLUMNS)
    return (
        dense_master_new,
        dense_first_new,
        dense_second_new,
        dense_weights,
        routed_master_new,
        routed_first_new,
        routed_second_new,
        routed_weights.reshape(EXPERTS, N_EDP, FF),
    )


def solution(mesh):
    inner = Mesh(mesh.devices.reshape(SIZES), AXES)
    in_specs = (
        P(AXES, None),
        P(AXES, None),
        P(AXES),
        P(AXES, None),
        P(AXES, None),
        P(AXES, None),
        P(EDP, EP, None, None),
        P(EP, EDP, None),
        P(EP, EDP, None),
        P(EP, EDP, None),
    )
    out_specs = (
        P(AXES, None),
        P(AXES, None),
        P(AXES, None),
        P(),
        P(EP, EDP, None),
        P(EP, EDP, None),
        P(EP, EDP, None),
        P(EP, None, None),
    )
    return jax.shard_map(
        per_device, mesh=inner, in_specs=in_specs, out_specs=out_specs, check_vma=False
    )
```

```python
import math

import jax
import jax.numpy as jnp
from jax import lax
from jax.experimental import pallas as pl
from jax.experimental.pallas import tpu as pltpu
from jax.sharding import Mesh, PartitionSpec as P

beta_one = 0.9
beta_two = 0.95
learn_rate = 0.001
decay_rate = 0.1
epsilon = 1e-08

AXES = ("xh", "z", "core", "xl", "y")
SIZES = (2, 16, 2, 2, 4)
EP = ("xh", "z", "core")
EDP = ("xl", "y")
NEAR = ("xh", "xl", "y")
FAR = ("z",)
N_NEAR, N_FAR, N_EDP, N_CORE, N_XH, N_DEV = 16, 16, 8, 2, 2, 512
ROWS, COLUMNS, EXPERTS, FF = 512, 1536, 4, 2048
HALF = ROWS // 2
W = 512
N_DENSE, N_ROUTED = COLUMNS // W, FF // W
DENSE_ROWS = N_DENSE * N_FAR
PACKED_ROWS = DENSE_ROWS + N_ROUTED * EXPERTS
LANES = 128
PIECES = COLUMNS // LANES
PIECE_ROWS = 16
f32, bf16 = jnp.float32, jnp.bfloat16


def adamw_update(gradient, master, first_moment, second_moment):
    first_new = beta_one * first_moment + (1.0 - beta_one) * gradient
    second_new = beta_two * second_moment + (1.0 - beta_two) * gradient * gradient
    master_new = master - learn_rate * (
        first_new / (jnp.sqrt(second_new) + epsilon) + decay_rate * master
    )
    return (master_new, first_new, second_new)


def exchange(x, axes):
    return lax.all_to_all(x, axes, 0, 0, tiled=False)


def iota(shape, dim):
    return lax.broadcasted_iota(jnp.int32, shape, dim)


def call(kernel, out_shape, flops=0, nbytes=1 << 20, scratch=()):
    return pl.pallas_call(
        kernel,
        out_shape=out_shape,
        scratch_shapes=scratch,
        compiler_params=pltpu.CompilerParams(vmem_limit_bytes=24 << 20),
        cost_estimate=pl.CostEstimate(flops=flops, bytes_accessed=nbytes, transcendentals=0),
    )


def routed_pack_kernel(routed, out):
    xh = lax.axis_index("xh")
    shape = (N_NEAR * 16, EXPERTS * N_EDP)
    q, c = iota(shape, 0), iota(shape, 1)
    same = (q // 128 == xh) & (q // 16 % N_EDP == c % N_EDP) & (q % EXPERTS == c // N_EDP)
    total = jnp.zeros((N_NEAR * 16, W), f32)
    for b in range(N_ROUTED):
        pick = jnp.where(same & (q // EXPERTS % N_ROUTED == b), 1.0, 0.0).astype(bf16)
        total += jnp.dot(pick, routed[:, b * W : (b + 1) * W], preferred_element_type=f32)
    out[...] = total.astype(bf16).reshape(N_NEAR, 16, W)


def pack_kernel(own, received, routed, out):
    for i in range(N_DENSE):
        cols = slice(i * W, (i + 1) * W)
        s = own[:, cols] + received[:, cols].astype(f32)
        out[:, i * N_FAR : (i + 1) * N_FAR, :] = s.astype(bf16).reshape(N_NEAR, N_FAR, W)
    out[:, DENSE_ROWS:, :] = routed[...]


def middle_kernel(got, master, first, second, far_out, weights_out, routed_out):
    total = jnp.sum(got[...].astype(f32), axis=0)
    pieces = [
        total[i * N_FAR : (i + 1) * N_FAR, j * LANES : (j + 1) * LANES]
        for i in range(N_DENSE)
        for j in range(W // LANES)
    ]
    pieces += [jnp.zeros((N_FAR, LANES), f32)] * (PIECE_ROWS - PIECES)
    far_out[...] = jnp.swapaxes(jnp.stack(pieces, axis=0), 0, 1).astype(bf16)
    routed = total[DENSE_ROWS:]
    routed_out[...] = routed
    rows = [adamw_update(routed_row(routed, x), master[x], first[x], second[x])[0] for x in range(EXPERTS)]
    packed = [rows[x][:, b * W : (b + 1) * W] for b in range(N_ROUTED) for x in range(EXPERTS)]
    weights_out[...] = jnp.concatenate(packed, axis=0).astype(bf16)


def routed_row(routed, x):
    return jnp.concatenate(
        [routed[b * EXPERTS + x : b * EXPERTS + x + 1] for b in range(N_ROUTED)], axis=1
    )


def updated(factor, got, master, first, second):
    total = jnp.sum(got[...].astype(f32), axis=0)
    g = jnp.concatenate([total[k : k + 1] for k in range(PIECES)], axis=1) * factor
    return adamw_update(g, master[...], first[...], second[...])


def weights_kernel(factor, got, master, first, second, far_out):
    p = updated(factor, got, master, first, second)[0]
    pieces = [p[:, k * LANES : (k + 1) * LANES] for k in range(PIECES)]
    pieces += [jnp.zeros((PIECE_ROWS - PIECES, LANES), f32)]
    row = jnp.concatenate(pieces, axis=0).astype(bf16)
    far_out[...] = jnp.broadcast_to(row[None], far_out.shape)


def state_kernel(factor, got, master, first, second, routed, routed_master, routed_first, routed_second, *outs):
    master_out, first_out, second_out, routed_master_out, routed_first_out, routed_second_out = outs
    p, m, v = updated(factor, got, master, first, second)
    master_out[...], first_out[...], second_out[...] = p, m, v
    total = routed[...]
    for x in range(EXPERTS):
        p, m, v = adamw_update(
            routed_row(total, x), routed_master[x], routed_first[x], routed_second[x]
        )
        routed_master_out[x], routed_first_out[x], routed_second_out[x] = p, m, v


def spread_kernel(got, weights, out):
    rows = jnp.swapaxes(got[...].astype(f32), 0, 1)
    per = W // LANES
    blocks = [
        jnp.concatenate([rows[i * per + j] for j in range(per)], axis=1) for i in range(N_DENSE)
    ]
    block = jnp.concatenate(blocks, axis=0).astype(bf16)
    for d in range(N_NEAR):
        out[d, :DENSE_ROWS, :] = block
        out[d, DENSE_ROWS:, :] = weights[...]


def place_matrix():
    n = N_EDP * N_FAR
    p, q = iota((n, n), 0), iota((n, n), 1)
    same = (p // N_EDP == q % N_FAR) & (p % N_EDP == q // N_FAR)
    return jnp.where(same, 1.0, 0.0).astype(bf16)


def place_rows(packed, core, out, blocks, sems):
    n = N_EDP * N_FAR
    place = place_matrix()
    copies = []
    for x in range(N_XH):
        for i in range(N_DENSE):
            rows = packed[x * N_EDP : (x + 1) * N_EDP, i * N_FAR : (i + 1) * N_FAR, :]
            block = jnp.dot(place, rows.reshape(n, W), preferred_element_type=f32)
            k = x * N_DENSE + i
            blocks[k] = block.reshape(N_FAR, N_EDP, W).astype(bf16)
            to = out.at[pl.ds(x * N_FAR, N_FAR), core, :, pl.ds(i * W, W)]
            copies.append(pltpu.make_async_copy(blocks.at[k], to, sems.at[k]))
            copies[-1].start()
    return copies


def own_place_kernel(core, own, dense_out, routed_out):
    n = N_EDP * N_FAR
    place = place_matrix()
    for x in range(N_XH):
        for i in range(N_DENSE):
            rows = own[x * N_EDP : (x + 1) * N_EDP, i * N_FAR : (i + 1) * N_FAR, :]
            block = jnp.dot(place, rows.reshape(n, W), preferred_element_type=f32)
            dense_out[x * N_FAR : (x + 1) * N_FAR, 0, :, i * W : (i + 1) * W] = block.reshape(
                N_FAR, N_EDP, W
            ).astype(bf16)
    xh = lax.axis_index("xh")
    shape = (EXPERTS * N_EDP, N_NEAR * 16)
    c, q = iota(shape, 0), iota(shape, 1)
    same = (q // 128 == xh) & (q // 16 % N_EDP == c % N_EDP) & (q % EXPERTS == c // N_EDP)
    packed = own[:, DENSE_ROWS:, :].reshape(N_NEAR * 16, W)
    for b in range(N_ROUTED):
        pick = jnp.where(same & (q // EXPERTS % N_ROUTED == b), 1.0, 0.0).astype(bf16)
        routed_out[:, b * W : (b + 1) * W] = jnp.dot(
            pick, packed, preferred_element_type=f32
        ).astype(bf16)


def other_place_kernel(other, held, dense_out, blocks, sems):
    for copy in place_rows(other, 1 - lax.axis_index("core"), dense_out, blocks, sems):
        copy.wait()


def per_device(
    dense_acts,
    dense_cot,
    advantage,
    dense_master,
    dense_first,
    dense_second,
    routed_grads,
    routed_master,
    routed_first,
    routed_second,
):
    factor = 1.0 / math.sqrt(dense_acts.shape[0] * N_DEV)
    core = lax.axis_index("core")
    sds = jax.ShapeDtypeStruct

    packed = jnp.arange(ROWS)[None, :]
    which, xh, e, z = packed // HALF, packed // 128 % N_XH, packed // N_FAR % N_EDP, packed % N_FAR
    row = ((xh * N_FAR + z) * N_CORE + jnp.where(which == 1, core, 1 - core)) * N_EDP + e
    place = (jnp.arange(ROWS)[:, None] == row).astype(bf16)

    def picked(columns):
        return lax.optimization_barrier(
            lax.dot_general(
                dense_acts, columns, (((1,), (0,)), ((), ())), preferred_element_type=bf16
            )
        )

    scaled = (advantage[:, None] * dense_cot.astype(f32)).astype(bf16)

    def product(a):
        return lax.dot_general(a, scaled, (((0,), (0,)), ((), ())), preferred_element_type=f32)

    swap = [(0, 1), (1, 0)]
    received = lax.ppermute(product(picked(place[:, :HALF])).astype(bf16), "core", swap)
    own = product(picked(place[:, HALF:]))
    near = sds((N_NEAR, PACKED_ROWS, W), bf16)
    far = sds((N_FAR, PIECE_ROWS, LANES), bf16)
    rows_r = sds((EXPERTS, 1, FF), f32)
    rows_d = sds((1, COLUMNS), f32)
    routed_sent = call(routed_pack_kernel, sds((N_NEAR, 16, W), bf16), 64 << 20)(
        routed_grads.reshape(EXPERTS * N_EDP, FF)
    )
    sent = call(pack_kernel, near)(own, received, routed_sent)
    got = exchange(sent, NEAR)
    far_sent, weights, routed_total = call(
        middle_kernel, (far, sds((16, W), bf16), sds((16, W), f32))
    )(got, routed_master, routed_first, routed_second)
    got = exchange(far_sent, FAR)

    def ahead(*refs):
        weights_kernel(factor, *refs)

    def state(*refs):
        state_kernel(factor, *refs)

    dense_args = (got, dense_master, dense_first, dense_second)
    far_sent = call(ahead, far)(*dense_args)
    (
        dense_master_new,
        dense_first_new,
        dense_second_new,
        routed_master_new,
        routed_first_new,
        routed_second_new,
    ) = call(state, (rows_d, rows_d, rows_d, rows_r, rows_r, rows_r))(
        *dense_args, routed_total, routed_master, routed_first, routed_second
    )
    got = exchange(far_sent, FAR)
    own = exchange(call(spread_kernel, near)(got, weights), NEAR)
    other = lax.ppermute(own, "core", swap)
    dense_shape = sds((ROWS // 16, N_CORE, N_EDP, COLUMNS), bf16)
    anywhere = pl.BlockSpec(memory_space=pl.ANY)
    vmem = pl.BlockSpec(memory_space=pltpu.VMEM)
    n_blocks = N_XH * N_DENSE
    place_params = dict(
        scratch_shapes=[
            pltpu.VMEM((n_blocks, N_FAR, N_EDP, W), bf16),
            pltpu.SemaphoreType.DMA((n_blocks,)),
        ],
        compiler_params=pltpu.CompilerParams(vmem_limit_bytes=24 << 20),
        cost_estimate=pl.CostEstimate(flops=200 << 20, bytes_accessed=2 << 20, transcendentals=0),
    )
    held, routed_weights = pl.pallas_call(
        own_place_kernel,
        out_shape=(dense_shape, sds((EXPERTS * N_EDP, FF), bf16)),
        grid_spec=pltpu.PrefetchScalarGridSpec(
            num_scalar_prefetch=1,
            grid=(1,),
            in_specs=[pl.BlockSpec((N_NEAR, PACKED_ROWS, W), lambda i, c: (0, 0, 0))],
            out_specs=[
                pl.BlockSpec((ROWS // 16, 1, N_EDP, COLUMNS), lambda i, c: (0, c[0], 0, 0)),
                pl.BlockSpec((EXPERTS * N_EDP, FF), lambda i, c: (0, 0)),
            ],
        ),
        compiler_params=place_params["compiler_params"],
        cost_estimate=place_params["cost_estimate"],
    )(core[None], own)
    dense_weights = pl.pallas_call(
        other_place_kernel,
        in_specs=[vmem, anywhere],
        out_specs=anywhere,
        out_shape=dense_shape,
        input_output_aliases={1: 0},
        **place_params,
    )(other, held).reshape(ROWS, COLUMNS)
    return (
        dense_master_new,
        dense_first_new,
        dense_second_new,
        dense_weights,
        routed_master_new,
        routed_first_new,
        routed_second_new,
        routed_weights.reshape(EXPERTS, N_EDP, FF),
    )


def solution(mesh):
    inner = Mesh(mesh.devices.reshape(SIZES), AXES)
    in_specs = (
        P(AXES, None),
        P(AXES, None),
        P(AXES),
        P(AXES, None),
        P(AXES, None),
        P(AXES, None),
        P(EDP, EP, None, None),
        P(EP, EDP, None),
        P(EP, EDP, None),
        P(EP, EDP, None),
    )
    out_specs = (
        P(AXES, None),
        P(AXES, None),
        P(AXES, None),
        P(),
        P(EP, EDP, None),
        P(EP, EDP, None),
        P(EP, EDP, None),
        P(EP, None, None),
    )
    return jax.shard_map(
        per_device, mesh=inner, in_specs=in_specs, out_specs=out_specs, check_vma=False
    )
```

```python
import math

import jax
import jax.numpy as jnp
from jax import lax
from jax.experimental import pallas as pl
from jax.experimental.pallas import tpu as pltpu
from jax.sharding import Mesh, PartitionSpec as P

beta_one = 0.9
beta_two = 0.95
learn_rate = 0.001
decay_rate = 0.1
epsilon = 1e-08

AXES = ("xh", "z", "core", "xl", "y")
SIZES = (2, 16, 2, 2, 4)
EP = ("xh", "z", "core")
EDP = ("xl", "y")
NEAR = ("xl", "xh", "y")
FAR = ("z",)
N_NEAR, N_FAR, N_EDP, N_CORE, N_XH, N_DEV = 16, 16, 8, 2, 2, 512
ROWS, COLUMNS, EXPERTS, FF = 512, 1536, 4, 2048
HALF = ROWS // 2
W = 512
N_DENSE, N_ROUTED = COLUMNS // W, FF // W
DENSE_ROWS = N_DENSE * N_FAR
PACKED_ROWS = DENSE_ROWS + N_ROUTED * EXPERTS
LANES = 128
PIECES = COLUMNS // LANES
PIECE_ROWS = 16
f32, bf16 = jnp.float32, jnp.bfloat16


def adamw_update(gradient, master, first_moment, second_moment):
    first_new = beta_one * first_moment + (1.0 - beta_one) * gradient
    second_new = beta_two * second_moment + (1.0 - beta_two) * gradient * gradient
    master_new = master - learn_rate * (
        first_new / (jnp.sqrt(second_new) + epsilon) + decay_rate * master
    )
    return (master_new, first_new, second_new)


def exchange(x, axes):
    return lax.all_to_all(x, axes, 0, 0, tiled=False)


def chip(d):
    return d // 4 % N_XH, d // N_EDP * 4 + d % 4


def of_half(packed, x, i):
    rows = slice(i * N_FAR, (i + 1) * N_FAR)
    parts = [packed[at : at + 4, rows, :] for at in (x * 4, N_EDP + x * 4)]
    return jnp.concatenate(parts, axis=0).reshape(N_EDP * N_FAR, W)


def iota(shape, dim):
    return lax.broadcasted_iota(jnp.int32, shape, dim)


def call(kernel, out_shape, flops=0, nbytes=1 << 20, scratch=()):
    return pl.pallas_call(
        kernel,
        out_shape=out_shape,
        scratch_shapes=scratch,
        compiler_params=pltpu.CompilerParams(vmem_limit_bytes=24 << 20),
        cost_estimate=pl.CostEstimate(flops=flops, bytes_accessed=nbytes, transcendentals=0),
    )


def routed_pack_kernel(routed, out):
    xh = lax.axis_index("xh")
    shape = (N_NEAR * 16, EXPERTS * N_EDP)
    q, c = iota(shape, 0), iota(shape, 1)
    half, e = chip(q // 16)
    same = (half == xh) & (e == c % N_EDP) & (q % EXPERTS == c // N_EDP)
    total = jnp.zeros((N_NEAR * 16, W), f32)
    for b in range(N_ROUTED):
        pick = jnp.where(same & (q // EXPERTS % N_ROUTED == b), 1.0, 0.0).astype(bf16)
        total += jnp.dot(pick, routed[:, b * W : (b + 1) * W], preferred_element_type=f32)
    out[...] = total.astype(bf16).reshape(N_NEAR, 16, W)


def pack_kernel(own, received, routed, out):
    for i in range(N_DENSE):
        cols = slice(i * W, (i + 1) * W)
        s = own[:, cols] + received[:, cols].astype(f32)
        out[:, i * N_FAR : (i + 1) * N_FAR, :] = s.astype(bf16).reshape(N_NEAR, N_FAR, W)
    out[:, DENSE_ROWS:, :] = routed[...]


def middle_kernel(got, master, first, second, far_out, weights_out, routed_out):
    total = jnp.sum(got[...].astype(f32), axis=0)
    pieces = [
        total[i * N_FAR : (i + 1) * N_FAR, j * LANES : (j + 1) * LANES]
        for i in range(N_DENSE)
        for j in range(W // LANES)
    ]
    pieces += [jnp.zeros((N_FAR, LANES), f32)] * (PIECE_ROWS - PIECES)
    far_out[...] = jnp.swapaxes(jnp.stack(pieces, axis=0), 0, 1).astype(bf16)
    routed = total[DENSE_ROWS:]
    routed_out[...] = routed
    rows = [adamw_update(routed_row(routed, x), master[x], first[x], second[x])[0] for x in range(EXPERTS)]
    packed = [rows[x][:, b * W : (b + 1) * W] for b in range(N_ROUTED) for x in range(EXPERTS)]
    weights_out[...] = jnp.concatenate(packed, axis=0).astype(bf16)


def routed_row(routed, x):
    return jnp.concatenate(
        [routed[b * EXPERTS + x : b * EXPERTS + x + 1] for b in range(N_ROUTED)], axis=1
    )


def updated(factor, got, master, first, second):
    total = jnp.sum(got[...].astype(f32), axis=0)
    g = jnp.concatenate([total[k : k + 1] for k in range(PIECES)], axis=1) * factor
    return adamw_update(g, master[...], first[...], second[...])


def weights_kernel(factor, got, master, first, second, far_out):
    p = updated(factor, got, master, first, second)[0]
    pieces = [p[:, k * LANES : (k + 1) * LANES] for k in range(PIECES)]
    pieces += [jnp.zeros((PIECE_ROWS - PIECES, LANES), f32)]
    row = jnp.concatenate(pieces, axis=0).astype(bf16)
    far_out[...] = jnp.broadcast_to(row[None], far_out.shape)


def state_kernel(factor, got, master, first, second, routed, routed_master, routed_first, routed_second, *outs):
    master_out, first_out, second_out, routed_master_out, routed_first_out, routed_second_out = outs
    p, m, v = updated(factor, got, master, first, second)
    master_out[...], first_out[...], second_out[...] = p, m, v
    total = routed[...]
    for x in range(EXPERTS):
        p, m, v = adamw_update(
            routed_row(total, x), routed_master[x], routed_first[x], routed_second[x]
        )
        routed_master_out[x], routed_first_out[x], routed_second_out[x] = p, m, v


def spread_kernel(got, weights, out):
    rows = jnp.swapaxes(got[...].astype(f32), 0, 1)
    per = W // LANES
    blocks = [
        jnp.concatenate([rows[i * per + j] for j in range(per)], axis=1) for i in range(N_DENSE)
    ]
    block = jnp.concatenate(blocks, axis=0).astype(bf16)
    for d in range(N_NEAR):
        out[d, :DENSE_ROWS, :] = block
        out[d, DENSE_ROWS:, :] = weights[...]


def place_matrix():
    n = N_EDP * N_FAR
    p, q = iota((n, n), 0), iota((n, n), 1)
    same = (p // N_EDP == q % N_FAR) & (p % N_EDP == q // N_FAR)
    return jnp.where(same, 1.0, 0.0).astype(bf16)


def place_rows(packed, core, out, blocks, sems):
    place = place_matrix()
    copies = []
    for x in range(N_XH):
        for i in range(N_DENSE):
            block = jnp.dot(place, of_half(packed, x, i), preferred_element_type=f32)
            k = x * N_DENSE + i
            blocks[k] = block.reshape(N_FAR, N_EDP, W).astype(bf16)
            to = out.at[pl.ds(x * N_FAR, N_FAR), core, :, pl.ds(i * W, W)]
            copies.append(pltpu.make_async_copy(blocks.at[k], to, sems.at[k]))
            copies[-1].start()
    return copies


def own_place_kernel(core, own, dense_out, routed_out):
    place = place_matrix()
    for x in range(N_XH):
        for i in range(N_DENSE):
            block = jnp.dot(place, of_half(own, x, i), preferred_element_type=f32)
            dense_out[x * N_FAR : (x + 1) * N_FAR, 0, :, i * W : (i + 1) * W] = block.reshape(
                N_FAR, N_EDP, W
            ).astype(bf16)
    xh = lax.axis_index("xh")
    shape = (EXPERTS * N_EDP, N_NEAR * 16)
    c, q = iota(shape, 0), iota(shape, 1)
    half, e = chip(q // 16)
    same = (half == xh) & (e == c % N_EDP) & (q % EXPERTS == c // N_EDP)
    packed = own[:, DENSE_ROWS:, :].reshape(N_NEAR * 16, W)
    for b in range(N_ROUTED):
        pick = jnp.where(same & (q // EXPERTS % N_ROUTED == b), 1.0, 0.0).astype(bf16)
        routed_out[:, b * W : (b + 1) * W] = jnp.dot(
            pick, packed, preferred_element_type=f32
        ).astype(bf16)


def other_place_kernel(other, held, dense_out, blocks, sems):
    for copy in place_rows(other, 1 - lax.axis_index("core"), dense_out, blocks, sems):
        copy.wait()


def per_device(
    dense_acts,
    dense_cot,
    advantage,
    dense_master,
    dense_first,
    dense_second,
    routed_grads,
    routed_master,
    routed_first,
    routed_second,
):
    factor = 1.0 / math.sqrt(dense_acts.shape[0] * N_DEV)
    core = lax.axis_index("core")
    sds = jax.ShapeDtypeStruct

    packed = jnp.arange(ROWS)[None, :]
    which, z = packed // HALF, packed % N_FAR
    xh, e = chip(packed // N_FAR % N_NEAR)
    row = ((xh * N_FAR + z) * N_CORE + jnp.where(which == 1, core, 1 - core)) * N_EDP + e
    place = (jnp.arange(ROWS)[:, None] == row).astype(bf16)

    def picked(columns):
        return lax.optimization_barrier(
            lax.dot_general(
                dense_acts, columns, (((1,), (0,)), ((), ())), preferred_element_type=bf16
            )
        )

    scaled = (advantage[:, None] * dense_cot.astype(f32)).astype(bf16)

    def product(a):
        return lax.dot_general(a, scaled, (((0,), (0,)), ((), ())), preferred_element_type=f32)

    swap = [(0, 1), (1, 0)]
    received = lax.ppermute(product(picked(place[:, :HALF])).astype(bf16), "core", swap)
    own = product(picked(place[:, HALF:]))
    near = sds((N_NEAR, PACKED_ROWS, W), bf16)
    far = sds((N_FAR, PIECE_ROWS, LANES), bf16)
    rows_r = sds((EXPERTS, 1, FF), f32)
    rows_d = sds((1, COLUMNS), f32)
    routed_sent = call(routed_pack_kernel, sds((N_NEAR, 16, W), bf16), 64 << 20)(
        routed_grads.reshape(EXPERTS * N_EDP, FF)
    )
    sent = call(pack_kernel, near)(own, received, routed_sent)
    got = exchange(sent, NEAR)
    far_sent, weights, routed_total = call(
        middle_kernel, (far, sds((16, W), bf16), sds((16, W), f32))
    )(got, routed_master, routed_first, routed_second)
    got = exchange(far_sent, FAR)

    def ahead(*refs):
        weights_kernel(factor, *refs)

    def state(*refs):
        state_kernel(factor, *refs)

    dense_args = (got, dense_master, dense_first, dense_second)
    far_sent = call(ahead, far)(*dense_args)
    (
        dense_master_new,
        dense_first_new,
        dense_second_new,
        routed_master_new,
        routed_first_new,
        routed_second_new,
    ) = call(state, (rows_d, rows_d, rows_d, rows_r, rows_r, rows_r))(
        *dense_args, routed_total, routed_master, routed_first, routed_second
    )
    got = exchange(far_sent, FAR)
    own = exchange(call(spread_kernel, near)(got, weights), NEAR)
    other = lax.ppermute(own, "core", swap)
    dense_shape = sds((ROWS // 16, N_CORE, N_EDP, COLUMNS), bf16)
    anywhere = pl.BlockSpec(memory_space=pl.ANY)
    vmem = pl.BlockSpec(memory_space=pltpu.VMEM)
    n_blocks = N_XH * N_DENSE
    place_params = dict(
        scratch_shapes=[
            pltpu.VMEM((n_blocks, N_FAR, N_EDP, W), bf16),
            pltpu.SemaphoreType.DMA((n_blocks,)),
        ],
        compiler_params=pltpu.CompilerParams(vmem_limit_bytes=24 << 20),
        cost_estimate=pl.CostEstimate(flops=200 << 20, bytes_accessed=2 << 20, transcendentals=0),
    )
    held, routed_weights = pl.pallas_call(
        own_place_kernel,
        out_shape=(dense_shape, sds((EXPERTS * N_EDP, FF), bf16)),
        grid_spec=pltpu.PrefetchScalarGridSpec(
            num_scalar_prefetch=1,
            grid=(1,),
            in_specs=[pl.BlockSpec((N_NEAR, PACKED_ROWS, W), lambda i, c: (0, 0, 0))],
            out_specs=[
                pl.BlockSpec((ROWS // 16, 1, N_EDP, COLUMNS), lambda i, c: (0, c[0], 0, 0)),
                pl.BlockSpec((EXPERTS * N_EDP, FF), lambda i, c: (0, 0)),
            ],
        ),
        compiler_params=place_params["compiler_params"],
        cost_estimate=place_params["cost_estimate"],
    )(core[None], own)
    dense_weights = pl.pallas_call(
        other_place_kernel,
        in_specs=[vmem, anywhere],
        out_specs=anywhere,
        out_shape=dense_shape,
        input_output_aliases={1: 0},
        **place_params,
    )(other, held).reshape(ROWS, COLUMNS)
    return (
        dense_master_new,
        dense_first_new,
        dense_second_new,
        dense_weights,
        routed_master_new,
        routed_first_new,
        routed_second_new,
        routed_weights.reshape(EXPERTS, N_EDP, FF),
    )


def solution(mesh):
    inner = Mesh(mesh.devices.reshape(SIZES), AXES)
    in_specs = (
        P(AXES, None),
        P(AXES, None),
        P(AXES),
        P(AXES, None),
        P(AXES, None),
        P(AXES, None),
        P(EDP, EP, None, None),
        P(EP, EDP, None),
        P(EP, EDP, None),
        P(EP, EDP, None),
    )
    out_specs = (
        P(AXES, None),
        P(AXES, None),
        P(AXES, None),
        P(),
        P(EP, EDP, None),
        P(EP, EDP, None),
        P(EP, EDP, None),
        P(EP, None, None),
    )
    return jax.shard_map(
        per_device, mesh=inner, in_specs=in_specs, out_specs=out_specs, check_vma=False
    )
```

```python
import math

import jax
import jax.numpy as jnp
from jax import lax
from jax.experimental import pallas as pl
from jax.experimental.pallas import tpu as pltpu
from jax.sharding import Mesh, PartitionSpec as P

beta_one = 0.9
beta_two = 0.95
learn_rate = 0.001
decay_rate = 0.1
epsilon = 1e-08

AXES = ("xh", "zh", "zl", "core", "xl", "y")
SIZES = (2, 4, 4, 2, 2, 4)
EP = ("xh", "zh", "zl", "core")
EDP = ("xl", "y")
NEAR = ("xl", "xh", "y")
FAR = ("zl", "zh")
N_NEAR, N_FAR, N_EDP, N_CORE, N_XH, N_DEV = 16, 16, 8, 2, 2, 512
ROWS, COLUMNS, EXPERTS, FF = 512, 1536, 4, 2048
HALF = ROWS // 2
W = 512
N_DENSE, N_ROUTED = COLUMNS // W, FF // W
DENSE_ROWS = N_DENSE * N_FAR
PACKED_ROWS = DENSE_ROWS + N_ROUTED * EXPERTS
LANES = 128
PIECES = COLUMNS // LANES
PIECE_ROWS = 16
f32, bf16 = jnp.float32, jnp.bfloat16


def adamw_update(gradient, master, first_moment, second_moment):
    first_new = beta_one * first_moment + (1.0 - beta_one) * gradient
    second_new = beta_two * second_moment + (1.0 - beta_two) * gradient * gradient
    master_new = master - learn_rate * (
        first_new / (jnp.sqrt(second_new) + epsilon) + decay_rate * master
    )
    return (master_new, first_new, second_new)


def exchange(x, axes):
    return lax.all_to_all(x, axes, 0, 0, tiled=False)


def chip(d):
    return d // 4 % N_XH, d // N_EDP * 4 + d % 4


def level(p):
    return p % 4 * 4 + p // 4


def of_half(packed, x, i):
    rows = slice(i * N_FAR, (i + 1) * N_FAR)
    parts = [packed[at : at + 4, rows, :] for at in (x * 4, N_EDP + x * 4)]
    return jnp.concatenate(parts, axis=0).reshape(N_EDP * N_FAR, W)


def iota(shape, dim):
    return lax.broadcasted_iota(jnp.int32, shape, dim)


def call(kernel, out_shape, flops=0, nbytes=1 << 20, scratch=()):
    return pl.pallas_call(
        kernel,
        out_shape=out_shape,
        scratch_shapes=scratch,
        compiler_params=pltpu.CompilerParams(vmem_limit_bytes=24 << 20),
        cost_estimate=pl.CostEstimate(flops=flops, bytes_accessed=nbytes, transcendentals=0),
    )


def routed_pack_kernel(routed, out):
    xh = lax.axis_index("xh")
    shape = (N_NEAR * 16, EXPERTS * N_EDP)
    q, c = iota(shape, 0), iota(shape, 1)
    half, e = chip(q // 16)
    same = (half == xh) & (e == c % N_EDP) & (q % EXPERTS == c // N_EDP)
    total = jnp.zeros((N_NEAR * 16, W), f32)
    for b in range(N_ROUTED):
        pick = jnp.where(same & (q // EXPERTS % N_ROUTED == b), 1.0, 0.0).astype(bf16)
        total += jnp.dot(pick, routed[:, b * W : (b + 1) * W], preferred_element_type=f32)
    out[...] = total.astype(bf16).reshape(N_NEAR, 16, W)


def pack_kernel(own, received, routed, out):
    for i in range(N_DENSE):
        cols = slice(i * W, (i + 1) * W)
        s = own[:, cols] + received[:, cols].astype(f32)
        out[:, i * N_FAR : (i + 1) * N_FAR, :] = s.astype(bf16).reshape(N_NEAR, N_FAR, W)
    out[:, DENSE_ROWS:, :] = routed[...]


def middle_kernel(got, master, first, second, far_out, weights_out, routed_out):
    total = jnp.sum(got[...].astype(f32), axis=0)
    pieces = [
        total[i * N_FAR : (i + 1) * N_FAR, j * LANES : (j + 1) * LANES]
        for i in range(N_DENSE)
        for j in range(W // LANES)
    ]
    pieces += [jnp.zeros((N_FAR, LANES), f32)] * (PIECE_ROWS - PIECES)
    far_out[...] = jnp.swapaxes(jnp.stack(pieces, axis=0), 0, 1).astype(bf16)
    routed = total[DENSE_ROWS:]
    routed_out[...] = routed
    rows = [adamw_update(routed_row(routed, x), master[x], first[x], second[x])[0] for x in range(EXPERTS)]
    packed = [rows[x][:, b * W : (b + 1) * W] for b in range(N_ROUTED) for x in range(EXPERTS)]
    weights_out[...] = jnp.concatenate(packed, axis=0).astype(bf16)


def routed_row(routed, x):
    return jnp.concatenate(
        [routed[b * EXPERTS + x : b * EXPERTS + x + 1] for b in range(N_ROUTED)], axis=1
    )


def updated(factor, got, master, first, second):
    total = jnp.sum(got[...].astype(f32), axis=0)
    g = jnp.concatenate([total[k : k + 1] for k in range(PIECES)], axis=1) * factor
    return adamw_update(g, master[...], first[...], second[...])


def weights_kernel(factor, got, master, first, second, far_out):
    p = updated(factor, got, master, first, second)[0]
    pieces = [p[:, k * LANES : (k + 1) * LANES] for k in range(PIECES)]
    pieces += [jnp.zeros((PIECE_ROWS - PIECES, LANES), f32)]
    row = jnp.concatenate(pieces, axis=0).astype(bf16)
    far_out[...] = jnp.broadcast_to(row[None], far_out.shape)


def state_kernel(factor, got, master, first, second, routed, routed_master, routed_first, routed_second, *outs):
    master_out, first_out, second_out, routed_master_out, routed_first_out, routed_second_out = outs
    p, m, v = updated(factor, got, master, first, second)
    master_out[...], first_out[...], second_out[...] = p, m, v
    total = routed[...]
    for x in range(EXPERTS):
        p, m, v = adamw_update(
            routed_row(total, x), routed_master[x], routed_first[x], routed_second[x]
        )
        routed_master_out[x], routed_first_out[x], routed_second_out[x] = p, m, v


def spread_kernel(got, weights, out):
    rows = jnp.swapaxes(got[...].astype(f32), 0, 1)
    per = W // LANES
    blocks = [
        jnp.concatenate([rows[i * per + j] for j in range(per)], axis=1) for i in range(N_DENSE)
    ]
    block = jnp.concatenate(blocks, axis=0).astype(bf16)
    for d in range(N_NEAR):
        out[d, :DENSE_ROWS, :] = block
        out[d, DENSE_ROWS:, :] = weights[...]


def place_matrix():
    n = N_EDP * N_FAR
    p, q = iota((n, n), 0), iota((n, n), 1)
    same = (p // N_EDP == level(q % N_FAR)) & (p % N_EDP == q // N_FAR)
    return jnp.where(same, 1.0, 0.0).astype(bf16)


def place_rows(packed, core, out, blocks, sems):
    place = place_matrix()
    copies = []
    for x in range(N_XH):
        for i in range(N_DENSE):
            block = jnp.dot(place, of_half(packed, x, i), preferred_element_type=f32)
            k = x * N_DENSE + i
            blocks[k] = block.reshape(N_FAR, N_EDP, W).astype(bf16)
            to = out.at[pl.ds(x * N_FAR, N_FAR), core, :, pl.ds(i * W, W)]
            copies.append(pltpu.make_async_copy(blocks.at[k], to, sems.at[k]))
            copies[-1].start()
    return copies


def own_place_kernel(core, own, dense_out, routed_out):
    place = place_matrix()
    for x in range(N_XH):
        for i in range(N_DENSE):
            block = jnp.dot(place, of_half(own, x, i), preferred_element_type=f32)
            dense_out[x * N_FAR : (x + 1) * N_FAR, 0, :, i * W : (i + 1) * W] = block.reshape(
                N_FAR, N_EDP, W
            ).astype(bf16)
    xh = lax.axis_index("xh")
    shape = (EXPERTS * N_EDP, N_NEAR * 16)
    c, q = iota(shape, 0), iota(shape, 1)
    half, e = chip(q // 16)
    same = (half == xh) & (e == c % N_EDP) & (q % EXPERTS == c // N_EDP)
    packed = own[:, DENSE_ROWS:, :].reshape(N_NEAR * 16, W)
    for b in range(N_ROUTED):
        pick = jnp.where(same & (q // EXPERTS % N_ROUTED == b), 1.0, 0.0).astype(bf16)
        routed_out[:, b * W : (b + 1) * W] = jnp.dot(
            pick, packed, preferred_element_type=f32
        ).astype(bf16)


def other_place_kernel(other, held, dense_out, blocks, sems):
    for copy in place_rows(other, 1 - lax.axis_index("core"), dense_out, blocks, sems):
        copy.wait()


def per_device(
    dense_acts,
    dense_cot,
    advantage,
    dense_master,
    dense_first,
    dense_second,
    routed_grads,
    routed_master,
    routed_first,
    routed_second,
):
    factor = 1.0 / math.sqrt(dense_acts.shape[0] * N_DEV)
    core = lax.axis_index("core")
    sds = jax.ShapeDtypeStruct

    packed = jnp.arange(ROWS)[None, :]
    which, z = packed // HALF, level(packed % N_FAR)
    xh, e = chip(packed // N_FAR % N_NEAR)
    row = ((xh * N_FAR + z) * N_CORE + jnp.where(which == 1, core, 1 - core)) * N_EDP + e
    place = (jnp.arange(ROWS)[:, None] == row).astype(bf16)

    def picked(columns):
        return lax.optimization_barrier(
            lax.dot_general(
                dense_acts, columns, (((1,), (0,)), ((), ())), preferred_element_type=bf16
            )
        )

    scaled = (advantage[:, None] * dense_cot.astype(f32)).astype(bf16)

    def product(a):
        return lax.dot_general(a, scaled, (((0,), (0,)), ((), ())), preferred_element_type=f32)

    swap = [(0, 1), (1, 0)]
    received = lax.ppermute(product(picked(place[:, :HALF])).astype(bf16), "core", swap)
    own = product(picked(place[:, HALF:]))
    near = sds((N_NEAR, PACKED_ROWS, W), bf16)
    far = sds((N_FAR, PIECE_ROWS, LANES), bf16)
    rows_r = sds((EXPERTS, 1, FF), f32)
    rows_d = sds((1, COLUMNS), f32)
    routed_sent = call(routed_pack_kernel, sds((N_NEAR, 16, W), bf16), 64 << 20)(
        routed_grads.reshape(EXPERTS * N_EDP, FF)
    )
    sent = call(pack_kernel, near)(own, received, routed_sent)
    got = exchange(sent, NEAR)
    far_sent, weights, routed_total = call(
        middle_kernel, (far, sds((16, W), bf16), sds((16, W), f32))
    )(got, routed_master, routed_first, routed_second)
    got = exchange(far_sent, FAR)

    def ahead(*refs):
        weights_kernel(factor, *refs)

    def state(*refs):
        state_kernel(factor, *refs)

    dense_args = (got, dense_master, dense_first, dense_second)
    far_sent = call(ahead, far)(*dense_args)
    (
        dense_master_new,
        dense_first_new,
        dense_second_new,
        routed_master_new,
        routed_first_new,
        routed_second_new,
    ) = call(state, (rows_d, rows_d, rows_d, rows_r, rows_r, rows_r))(
        *dense_args, routed_total, routed_master, routed_first, routed_second
    )
    got = exchange(far_sent, FAR)
    own = exchange(call(spread_kernel, near)(got, weights), NEAR)
    other = lax.ppermute(own, "core", swap)
    dense_shape = sds((ROWS // 16, N_CORE, N_EDP, COLUMNS), bf16)
    anywhere = pl.BlockSpec(memory_space=pl.ANY)
    vmem = pl.BlockSpec(memory_space=pltpu.VMEM)
    n_blocks = N_XH * N_DENSE
    place_params = dict(
        scratch_shapes=[
            pltpu.VMEM((n_blocks, N_FAR, N_EDP, W), bf16),
            pltpu.SemaphoreType.DMA((n_blocks,)),
        ],
        compiler_params=pltpu.CompilerParams(vmem_limit_bytes=24 << 20),
        cost_estimate=pl.CostEstimate(flops=200 << 20, bytes_accessed=2 << 20, transcendentals=0),
    )
    held, routed_weights = pl.pallas_call(
        own_place_kernel,
        out_shape=(dense_shape, sds((EXPERTS * N_EDP, FF), bf16)),
        grid_spec=pltpu.PrefetchScalarGridSpec(
            num_scalar_prefetch=1,
            grid=(1,),
            in_specs=[pl.BlockSpec((N_NEAR, PACKED_ROWS, W), lambda i, c: (0, 0, 0))],
            out_specs=[
                pl.BlockSpec((ROWS // 16, 1, N_EDP, COLUMNS), lambda i, c: (0, c[0], 0, 0)),
                pl.BlockSpec((EXPERTS * N_EDP, FF), lambda i, c: (0, 0)),
            ],
        ),
        compiler_params=place_params["compiler_params"],
        cost_estimate=place_params["cost_estimate"],
    )(core[None], own)
    dense_weights = pl.pallas_call(
        other_place_kernel,
        in_specs=[vmem, anywhere],
        out_specs=anywhere,
        out_shape=dense_shape,
        input_output_aliases={1: 0},
        **place_params,
    )(other, held).reshape(ROWS, COLUMNS)
    return (
        dense_master_new,
        dense_first_new,
        dense_second_new,
        dense_weights,
        routed_master_new,
        routed_first_new,
        routed_second_new,
        routed_weights.reshape(EXPERTS, N_EDP, FF),
    )


def solution(mesh):
    inner = Mesh(mesh.devices.reshape(SIZES), AXES)
    in_specs = (
        P(AXES, None),
        P(AXES, None),
        P(AXES),
        P(AXES, None),
        P(AXES, None),
        P(AXES, None),
        P(EDP, EP, None, None),
        P(EP, EDP, None),
        P(EP, EDP, None),
        P(EP, EDP, None),
    )
    out_specs = (
        P(AXES, None),
        P(AXES, None),
        P(AXES, None),
        P(),
        P(EP, EDP, None),
        P(EP, EDP, None),
        P(EP, EDP, None),
        P(EP, None, None),
    )
    return jax.shard_map(
        per_device, mesh=inner, in_specs=in_specs, out_specs=out_specs, check_vma=False
    )
```
